32 devices in a mesh: chord: 4 (over y, core), span: 2 (over x), wall: 4 (over z).
Axes of the slice: x: 2, y: 2, z: 4, core: 2. Of those that a mesh axis runs over, the one named last changes fastest.
Arguments:
- sensitivity: float32 [6, 32, 32, 512], P(None, 'chord', 'span', 'wall'), may hold values from -6 to 6
- diagonal: float32 [6, 32, 32, 512], P(None, 'chord', 'span', 'wall'), may hold values from 10 to 20
- face_coef: float32 [3, 32, 32, 512], P(None, 'chord', 'span', 'wall'), may hold values from 0.3 to 1.5
- upper_blocks: float32 [3, 6, 6], replicated, may hold values from -2.5 to 2.5
- lower_blocks: float32 [3, 6, 6], replicated, may hold values from -2.5 to 2.5
- iface_blocks: float32 [2, 6, 6], replicated, may hold values from -2.5 to 2.5
- production: float32 [32, 32, 512], P('chord', 'span', 'wall'), may hold values from -6 to 6
- send_cell: int32 [4, 2, 4, 2, 64], P('chord', 'span', 'wall'), may hold values from 0 to 16383
- target_cell: int32 [4, 2, 4, 2, 64], P('chord', 'span', 'wall'), may hold values from 0 to 16383
- orient: int32 [4, 2, 4, 2, 64], P('chord', 'span', 'wall'), may hold values from 0 to 1
- iface_weight: float32 [4, 2, 4, 2, 64], P('chord', 'span', 'wall'), may hold values from 0.5 to 2
Outputs:
- adjoint: float32 [6, 32, 32, 512], P(None, 'chord', 'span', 'wall')
- gradient: float32 [32, 32, 512], P('chord', 'span', 'wall')
The draws below stay inside these ranges and needn't reach their ends.
All inputs are finite; a program needn't handle non-finite values.
Results may differ from the reference program's by a relative error of at most 0.0001.
Values sent between devices are 32-bit elements; how exact they have to be, the bound alone decides.
A program may use at most 64 MiB of HBM per device.

```python
import math
import jax
import jax.numpy as jnp
from jax import lax

NV = 6
CX = 8
CY = 16
CZ = 128
CAP = 64
SWEEPS = 3
NX = 32
NY = 32
NZ = 512
CELLS = 16384
N_CHORD = 4
N_SPAN = 2
N_WALL = 4


def set_ends(values, stream_key, least, largest):
    shape = values.shape
    place = [jax.random.randint(jax.random.fold_in(stream_key, axis), (), 0, shape[axis]) for axis in range(len(shape))]
    values = values.at[tuple(place)].set(least)
    longest = shape.index(max(shape))
    place[longest] = (place[longest] + 1) % shape[longest]
    return values.at[tuple(place)].set(largest)


def level_of(rng, dims, shards, low, top_value):
    def one(position, shards_of):
        draws = jax.random.uniform(jax.random.fold_in(jax.random.fold_in(rng, 6), position), (shards_of,), jnp.float32, low / len(shards), top_value / len(shards))
        return jnp.repeat(jnp.exp(draws), dims[position] // shards_of).reshape((-1,) + (1,) * (len(dims) - position - 1))

    level = one(*shards[0])
    for cut in shards[1:]:
        level = level * one(*cut)
    return level


def gaussian(own_key, shape, deviation, limit, cuts=(), held_as=jnp.bfloat16):
    loudness = level_of(own_key, shape, cuts, -0.22, 0.18) if cuts else 1.0
    values = jax.random.normal(own_key, shape, jnp.float32) * deviation * loudness
    return jnp.minimum(jnp.maximum(values, -limit), limit).astype(held_as)


def setup_inputs(seed: int = 0) -> dict:
    key_of = jax.random.split(jax.random.key(seed), 12)
    sensitivity = gaussian(key_of[0], (NV, NX, NY, NZ), 1.0, 6.0, ((1, 4), (2, 2), (3, 4)), jnp.float32)
    diagonal = jnp.clip(jnp.exp(math.log(20.0) - 0.6931472 * jax.random.uniform(key_of[1], (NV, NX, NY, NZ), jnp.float32) ** level_of(key_of[1], (NV, NX, NY, NZ), ((1, 4), (2, 2), (3, 4)), -0.2, 0.2)), 10.0, 20.0)
    face_coef = jnp.clip(0.3 + 1.2 * jax.random.uniform(key_of[2], (3, NX, NY, NZ), jnp.float32) ** level_of(key_of[2], (3, NX, NY, NZ), ((1, 4), (2, 2), (3, 4)), -0.2, 0.2), 0.3, 1.5)
    upper_blocks = gaussian(key_of[3], (3, NV, NV), NV ** -0.5, 2.5, (), jnp.float32)
    lower_blocks = gaussian(key_of[4], (3, NV, NV), NV ** -0.5, 2.5, (), jnp.float32)
    iface_blocks = gaussian(key_of[5], (2, NV, NV), NV ** -0.5, 2.5, (), jnp.float32)
    production = gaussian(key_of[6], (NX, NY, NZ), 1.0, 6.0, ((0, 4), (1, 2), (2, 4)), jnp.float32)
    send_cell = set_ends(jax.random.randint(key_of[7], (N_CHORD, N_SPAN, N_WALL, N_SPAN, CAP), 0, CELLS), jax.random.fold_in(key_of[7], 1), 0, CELLS - 1).astype(jnp.int32)
    target_cell = set_ends(jax.random.randint(key_of[8], (N_CHORD, N_SPAN, N_WALL, N_SPAN, CAP), 0, CELLS), jax.random.fold_in(key_of[8], 1), 0, CELLS - 1).astype(jnp.int32)
    orient = set_ends(jax.random.randint(key_of[9], (N_CHORD, N_SPAN, N_WALL, N_SPAN, CAP), 0, 2), jax.random.fold_in(key_of[9], 1), 0, 1).astype(jnp.int32)
    iface_weight = jnp.clip(jnp.exp(math.log(2.0) - 1.3862944 * jax.random.uniform(key_of[10], (N_CHORD, N_SPAN, N_WALL, N_SPAN, CAP), jnp.float32) ** level_of(key_of[10], (N_CHORD, N_SPAN, N_WALL, N_SPAN, CAP), ((0, 4), (1, 2), (2, 4)), -0.2, 0.2)), 0.5, 2.0)
    return dict(sensitivity=sensitivity, diagonal=diagonal, face_coef=face_coef, upper_blocks=upper_blocks, lower_blocks=lower_blocks, iface_blocks=iface_blocks, production=production, send_cell=send_cell, target_cell=target_cell, orient=orient, iface_weight=iface_weight)


def couple(block, field):
    return jnp.einsum('ji,jxyz->ixyz', block, field, precision=lax.Precision.HIGHEST)


def local_part(adjoint, diagonal, face_coef, upper_blocks, lower_blocks):
    padded = jnp.pad(adjoint, ((0, 0), (1, 1), (1, 1), (1, 1)))
    pairs = [(padded[:, 2:, 1:-1, 1:-1], padded[:, :-2, 1:-1, 1:-1]),
             (padded[:, 1:-1, 2:, 1:-1], padded[:, 1:-1, :-2, 1:-1]),
             (padded[:, 1:-1, 1:-1, 2:], padded[:, 1:-1, 1:-1, :-2])]
    result = diagonal * adjoint
    for axis_num in range(3):
        upper, lower = pairs[axis_num]
        result = result + face_coef[axis_num][None] * (couple(upper_blocks[axis_num], upper) + couple(lower_blocks[axis_num], lower))
    return result


def iface_part(adjoint, send_cell, target_cell, orient, iface_weight, iface_blocks):
    n_c, n_s, n_w = N_CHORD, N_SPAN, N_WALL
    cells = CX * CY * CZ
    blocks = adjoint.reshape(NV, n_c, CX, n_s, CY, n_w, CZ).transpose(0, 1, 3, 5, 2, 4, 6).reshape(NV, n_c, n_s, n_w, cells)
    source = jnp.take_along_axis(blocks, send_cell.reshape(1, n_c, n_s, n_w, n_s * CAP), axis=4).reshape(NV, n_c, n_s, n_w, n_s, CAP)
    first = jnp.einsum('ji,jabcdk->iabcdk', iface_blocks[0], source, precision=lax.Precision.HIGHEST)
    second = jnp.einsum('ji,jabcdk->iabcdk', iface_blocks[1], source, precision=lax.Precision.HIGHEST)
    values = jnp.where(orient[None] == 1, second, first) * iface_weight[None]
    shape = (n_c, n_s, n_w, n_s, CAP)
    chord_idx = lax.broadcasted_iota(jnp.int32, shape, 0)
    dest_idx = lax.broadcasted_iota(jnp.int32, shape, 3)
    wall_idx = lax.broadcasted_iota(jnp.int32, shape, 2)
    total = jnp.zeros((NV, n_c, n_s, n_w, cells), jnp.float32)
    total = total.at[:, chord_idx, dest_idx, wall_idx, target_cell.astype(jnp.int32)].add(values)
    return total.reshape(NV, n_c, n_s, n_w, CX, CY, CZ).transpose(0, 1, 4, 2, 5, 3, 6).reshape(NV, n_c * CX, n_s * CY, n_w * CZ)


def reference(sensitivity, diagonal, face_coef, upper_blocks, lower_blocks, iface_blocks, production, send_cell, target_cell, orient, iface_weight):
    adjoint = sensitivity / diagonal
    for sweep in range(SWEEPS):
        applied = local_part(adjoint, diagonal, face_coef, upper_blocks, lower_blocks) + iface_part(adjoint, send_cell, target_cell, orient, iface_weight, iface_blocks)
        adjoint = adjoint + (sensitivity - applied) / diagonal
    gradient = production * adjoint[NV - 1]
    return adjoint, gradient
```

```python
import functools

import jax
import jax.numpy as jnp
from jax import lax
from jax.experimental import pallas as pl
from jax.experimental.pallas import tpu as pltpu
from jax.sharding import PartitionSpec as P

SWEEPS = 3
LANES = 128
STEP = 2
MESH = pl.DeviceIdType.MESH
F32 = jnp.float32
BF16 = jnp.bfloat16


def iota(shape, dim):
    return lax.broadcasted_iota(jnp.int32, shape, dim)


def fiota(shape, dim):
    return iota(shape, dim).astype(F32)


def column(row, n):
    wide = jnp.broadcast_to(row.astype(F32), (n, n))
    return jnp.sum(jnp.where(iota((n, n), 0) == iota((n, n), 1), wide, 0.0), axis=1, keepdims=True)


def one_hots(cell):
    row = jnp.floor(cell * (1.0 / LANES))
    lane = fiota(cell.shape, 1)
    return jnp.where(row == lane, 1.0, 0.0), jnp.where(cell - row * LANES == lane, 1.0, 0.0)


def kernel(
    n_chord, n_span, n_wall, nv, cx, cy, slots,
    sens_hbm, diag_hbm, face_hbm, up_ref, low_ref, couple_ref, prod_hbm,
    send_ref, target_ref, orient_ref, weight_ref,
    out_ref, grad_ref,
    sens, rdiag, face, prod, adj, acc, halves,
    wall_out, wall_in, span_out, span_in, chord_in, span_term, wall_coef,
    iface_out, iface_in, cell_out, cell_in,
    pick_rows, pick_lanes, weights, put_rows, put_lanes, put_vals, put,
    load_sem, halo_send, halo_recv, iface_send, iface_recv, cell_send, cell_recv,
):
    total = n_span * slots
    chunks = cx // STEP
    ci, si, wi = lax.axis_index("chord"), lax.axis_index("span"), lax.axis_index("wall")
    places = (("chord", ci, n_chord), ("span", si, n_span), ("wall", wi, n_wall))

    def exists(axis, side):
        _, place, count = places[axis]
        return place > 0 if side == 0 else place < count - 1

    def neighbour(axis, side):
        name, place, _ = places[axis]
        return {name: place - 1 if side == 0 else place + 1}

    loads = [
        pltpu.make_async_copy(src, dst, load_sem.at[k])
        for k, (src, dst) in enumerate(
            ((sens_hbm, sens), (diag_hbm, rdiag), (face_hbm, face), (prod_hbm, prod))
        )
    ]
    for load in loads:
        load.start()

    barrier = pltpu.get_barrier_semaphore()
    for axis in (0, 2):
        for side in (0, 1):
            @pl.when(exists(axis, side))
            def _():
                pl.semaphore_signal(
                    barrier, inc=1, device_id=neighbour(axis, side), device_id_type=MESH
                )
    peers = [lax.rem(si + d, n_span) for d in range(1, n_span)]
    for peer in peers:
        pl.semaphore_signal(barrier, inc=1, device_id={"span": peer}, device_id_type=MESH)

    lane_id = iota((1, LANES), 1)
    for shift in range(-(nv - 1), nv):
        coef = jnp.zeros((1, LANES), F32)
        for i in range(nv):
            j = i + shift
            if 0 <= j < nv:
                mine = lane_id // (2 * cx) == i
                coef = jnp.where(mine & (lane_id % 2 == 0), up_ref[2, j, i], coef)
                coef = jnp.where(mine & (lane_id % 2 == 1), low_ref[2, j, i], coef)
        wall_coef[shift + nv - 1] = coef
    for buf in range(SWEEPS):
        for j in range(nv):
            adj[buf, j, 0] = jnp.zeros((cy, LANES), F32)
            adj[buf, j, cx + 1] = jnp.zeros((cy, LANES), F32)
    for sweep in range(SWEEPS):
        for side in (0, 1):
            @pl.when(jnp.logical_not(exists(0, side)))
            def _():
                chord_in[sweep, side] = jnp.zeros(chord_in.shape[2:], F32)

            @pl.when(jnp.logical_not(exists(1, side)))
            def _():
                span_in[sweep, side] = jnp.zeros(span_in.shape[2:], F32)

            @pl.when(jnp.logical_not(exists(2, side)))
            def _():
                wall_in[sweep, side] = jnp.zeros(wall_in.shape[2:], F32)

    table = []
    for o in range(2):
        rows = []
        for j in range(nv):
            row = jnp.zeros((1, LANES), F32)
            for i in range(nv):
                row = jnp.where(lane_id == i, couple_ref[o, j, i], row)
            rows.append(row)
        table.append(rows)
    send_all = send_ref[0, 0, 0]
    target_all = target_ref[0, 0, 0]
    orient_all = orient_ref[0, 0, 0]
    weight_all = weight_ref[0, 0, 0]
    for t in range(n_span):
        part = pl.ds(t * slots, slots)
        cell_out[t] = jnp.broadcast_to(column(target_all[t : t + 1], slots), (slots, LANES))
        cell = jnp.broadcast_to(column(send_all[t : t + 1], slots), (slots, LANES))
        rows, lanes = one_hots(cell)
        pick_rows[part, 0:LANES] = rows.astype(BF16)
        pick_rows[part, LANES : 2 * LANES] = rows.astype(BF16)
        pick_lanes[part] = lanes
        facing = column(orient_all[t : t + 1], slots)
        weight = column(weight_all[t : t + 1], slots)
        for j in range(nv):
            weights[j, part] = weight * jnp.where(facing == 1.0, table[1][j], table[0][j])

    greeted = n_span - 1
    for axis in (0, 2):
        for side in (0, 1):
            greeted = greeted + jnp.where(exists(axis, side), 1, 0)
    pl.semaphore_wait(barrier, greeted)

    def cell_copy(peer, slot):
        return pltpu.make_async_remote_copy(
            src_ref=cell_out.at[peer], dst_ref=cell_in.at[slot],
            send_sem=cell_send.at[peer], recv_sem=cell_recv.at[slot],
            device_id={"span": peer}, device_id_type=MESH,
        )

    for peer in peers:
        cell_copy(peer, si).start()
    cell_in[si] = cell_out[si]

    def halo_copy(sweep, axis, side):
        if axis == 0:
            src = adj.at[sweep, :, 1 if side == 0 else cx]
            dst = chord_in.at[sweep, 1 - side]
        elif axis == 1:
            src, dst = span_out.at[sweep, side], span_in.at[sweep, 1 - side]
        else:
            src, dst = wall_out.at[sweep], wall_in.at[sweep, 1 - side]
        return pltpu.make_async_remote_copy(
            src_ref=src, dst_ref=dst,
            send_sem=halo_send.at[sweep, 2 * axis + side],
            recv_sem=halo_recv.at[sweep, 2 * axis + 1 - side],
            device_id=neighbour(axis, side), device_id_type=MESH,
        )

    def each_halo(sweep, act):
        for axis in range(3):
            for side in (0, 1):
                @pl.when(exists(axis, side))
                def _():
                    act(axis, side)

    def start_halos(sweep):
        each_halo(sweep, lambda axis, side: halo_copy(sweep, axis, side).start())

    def wait_halos(sweep):
        each_halo(sweep, lambda axis, side: halo_copy(sweep, axis, 1 - side).wait_recv())

    def iface_copy(sweep, peer, slot):
        return pltpu.make_async_remote_copy(
            src_ref=iface_out.at[sweep, peer], dst_ref=iface_in.at[sweep, slot],
            send_sem=iface_send.at[sweep, peer], recv_sem=iface_recv.at[sweep, slot],
            device_id={"span": peer}, device_id_type=MESH,
        )

    lanes2d = iota((cy, LANES), 1)
    rows2d = iota((cy, LANES), 0)

    def keep(sweep, i, q, plane, value, packed):
        adj[sweep, i, plane + 1] = value
        high = value.astype(BF16)
        at = pl.multiple_of(plane * cy, cy)
        wide = pl.ds((i % 2) * LANES, LANES)
        halves[i // 2, pl.ds(at, cy), wide] = high
        halves[i // 2, pl.ds(cx * cy + at, cy), wide] = (value - high.astype(F32)).astype(BF16)
        span_out[sweep, 0, i, pl.ds(plane, 1)] = value[0:1]
        span_out[sweep, 1, i, pl.ds(plane, 1)] = value[cy - 1 : cy]
        pair = i * cx + plane
        turned = pltpu.roll(value, 2 * pair + 1, 1)
        return jnp.where(lanes2d // 2 == pair, turned, packed)

    loads[0].wait()
    loads[1].wait()

    def first(chunk, packed):
        for i in range(nv):
            for q in range(STEP):
                plane = chunk * STEP + q
                inverse = 1.0 / rdiag[i, plane]
                rdiag[i, plane] = inverse
                packed = keep(0, i, q, plane, sens[i, plane] * inverse, packed)
        return packed

    wall_out[0] = lax.fori_loop(0, chunks, first, jnp.zeros((cy, LANES), F32))
    start_halos(0)
    loads[2].wait()

    for sweep in range(SWEEPS):
        values = jnp.zeros((total, LANES), F32)
        for pair in range(nv // 2):
            picked = jnp.dot(pick_rows[...], halves[pair], preferred_element_type=F32)
            for h in range(2):
                own = picked[:, h * LANES : (h + 1) * LANES] * pick_lanes[...]
                values = values + jnp.sum(own, axis=1, keepdims=True) * weights[2 * pair + h]
        for t in range(n_span):
            iface_out[sweep, t] = values[t * slots : (t + 1) * slots]
        for peer in peers:
            iface_copy(sweep, peer, si).start()
        iface_in[sweep, si] = iface_out[sweep, si]

        def own_part(chunk, carry):
            at = chunk * STEP
            for axis in range(3):
                sums = [None] * nv
                for j in range(nv):
                    if axis == 0:
                        low = adj[sweep, j, pl.ds(at, STEP)].reshape(STEP * cy, LANES)
                        up = adj[sweep, j, pl.ds(at + 2, STEP)].reshape(STEP * cy, LANES)
                    else:
                        here = adj[sweep, j, pl.ds(at + 1, STEP)]
                        if axis == 1:
                            low = jnp.concatenate([pltpu.roll(here[q], 1, 0) for q in range(STEP)])
                            up = jnp.concatenate(
                                [pltpu.roll(here[q], cy - 1, 0) for q in range(STEP)]
                            )
                        else:
                            here = here.reshape(STEP * cy, LANES)
                            low = pltpu.roll(here, 1, 1)
                            up = pltpu.roll(here, LANES - 1, 1)
                    for i in range(nv):
                        term = up_ref[axis, j, i] * up + low_ref[axis, j, i] * low
                        sums[i] = term if j == 0 else sums[i] + term
                scale = face[axis, pl.ds(at, STEP)].reshape(STEP * cy, LANES)
                for i in range(nv):
                    base = sens if axis == 0 else acc
                    rest = base[i, pl.ds(at, STEP)].reshape(STEP * cy, LANES) - scale * sums[i]
                    acc[i, pl.ds(at, STEP)] = rest.reshape(STEP, cy, LANES)
            return carry

        lax.fori_loop(0, chunks, own_part, 0)

        wait_halos(sweep)

        for side in (0, 1):
            blocks = low_ref if side == 0 else up_ref
            edge = 0 if side == 0 else cx - 1
            for i in range(nv):
                chord_sum = None
                span_sum = None
                for j in range(nv):
                    chord_new = blocks[0, j, i] * chord_in[sweep, side, j]
                    span_new = blocks[1, j, i] * (span_in[sweep, side, j] - span_out[sweep, 1 - side, j])
                    chord_sum = chord_new if j == 0 else chord_sum + chord_new
                    span_sum = span_new if j == 0 else span_sum + span_new
                acc[i, edge] = acc[i, edge] - face[0, edge] * chord_sum
                span_term[side, i] = span_sum
        from_low = pltpu.roll(wall_in[sweep, 0] - wall_out[sweep], 1, 1)
        from_high = pltpu.roll(wall_in[sweep, 1] - wall_out[sweep], LANES - 1, 1)
        edges = jnp.where(lanes2d % 2 == 0, from_high, from_low)
        wall_term = jnp.zeros((cy, LANES), F32)
        for shift in range(-(nv - 1), nv):
            moved = edges if shift == 0 else pltpu.roll(edges, (-2 * cx * shift) % LANES, 1)
            wall_term = wall_term + wall_coef[shift + nv - 1] * moved

        if sweep == 0:
            for peer in peers:
                cell_copy(peer, peer).wait_recv()
            rows, lanes = one_hots(cell_in[...].reshape(total, LANES))
            put_lanes[...] = lanes
            turned = jnp.transpose(rows).astype(BF16)
            put_rows[:, 0:total] = turned
            put_rows[:, total : 2 * total] = turned
        for peer in peers:
            iface_copy(sweep, peer, peer).wait_recv()
        arrived = iface_in[sweep].reshape(total, LANES)
        for i in range(nv):
            spread = arrived[:, i : i + 1] * put_lanes[...]
            high = spread.astype(BF16)
            wide = slice((i % 2) * LANES, (i % 2 + 1) * LANES)
            put_vals[i // 2, 0:total, wide] = high
            put_vals[i // 2, total : 2 * total, wide] = (spread - high.astype(F32)).astype(BF16)
        for pair in range(nv // 2):
            put[pair] = jnp.dot(put_rows[...], put_vals[pair], preferred_element_type=F32)

        def finish(chunk, packed):
            for q in range(STEP):
                plane = chunk * STEP + q
                at = pl.multiple_of(plane * cy, cy)
                for i in range(nv):
                    turn = lax.rem(2 * LANES - 1 - 2 * (i * cx + plane), LANES)
                    wall = pltpu.roll(wall_term, turn, 1)
                    wall = jnp.where((lanes2d == 0) | (lanes2d == LANES - 1), wall, 0.0)
                    span = jnp.where(rows2d == 0, span_term[0, i, pl.ds(plane, 1)], 0.0)
                    span = jnp.where(rows2d == cy - 1, span_term[1, i, pl.ds(plane, 1)], span)
                    rest = acc[i, plane] - face[1, plane] * span - face[2, plane] * wall
                    rest = rest - put[i // 2, pl.ds(at, cy), pl.ds((i % 2) * LANES, LANES)]
                    value = rest * rdiag[i, plane]
                    if sweep < SWEEPS - 1:
                        packed = keep(sweep + 1, i, q, plane, value, packed)
                    else:
                        out_ref[i, plane] = value
                        if i == nv - 1:
                            grad_ref[plane] = prod[plane] * value
            return packed

        if sweep == SWEEPS - 1:
            loads[3].wait()
        packed = lax.fori_loop(0, chunks, finish, jnp.zeros((cy, LANES), F32))
        if sweep < SWEEPS - 1:
            wall_out[sweep + 1] = packed
            start_halos(sweep + 1)

    for peer in peers:
        cell_copy(peer, si).wait_send()
    for sweep in range(SWEEPS):
        each_halo(sweep, lambda axis, side: halo_copy(sweep, axis, side).wait_send())
        for peer in peers:
            iface_copy(sweep, peer, si).wait_send()


def solution(mesh):
    n_chord, n_span, n_wall = mesh.shape["chord"], mesh.shape["span"], mesh.shape["wall"]

    def local(
        sensitivity, diagonal, face_coef, upper_blocks, lower_blocks, iface_blocks, production,
        send_cell, target_cell, orient, iface_weight,
    ):
        nv, cx, cy, cz = sensitivity.shape
        slots = send_cell.shape[-1]
        total = n_span * slots
        pairs = nv // 2
        vmem = pl.BlockSpec(memory_space=pltpu.VMEM)
        smem = pl.BlockSpec(memory_space=pltpu.SMEM)
        hbm = pl.BlockSpec(memory_space=pl.ANY)
        dma = pltpu.SemaphoreType.DMA
        field = (nv, cx, cy, cz)
        return pl.pallas_call(
            functools.partial(kernel, n_chord, n_span, n_wall, nv, cx, cy, slots),
            out_shape=(
                jax.ShapeDtypeStruct(field, F32),
                jax.ShapeDtypeStruct((cx, cy, cz), F32),
            ),
            in_specs=[hbm, hbm, hbm, smem, smem, smem, hbm, vmem, vmem, vmem, vmem],
            out_specs=(vmem, vmem),
            scratch_shapes=[
                pltpu.VMEM(field, F32),
                pltpu.VMEM(field, F32),
                pltpu.VMEM((3, cx, cy, cz), F32),
                pltpu.VMEM((cx, cy, cz), F32),
                pltpu.VMEM((SWEEPS, nv, cx + 2, cy, cz), F32),
                pltpu.VMEM(field, F32),
                pltpu.VMEM((pairs, 2 * cx * cy, 2 * cz), BF16),
                pltpu.VMEM((SWEEPS, cy, LANES), F32),
                pltpu.VMEM((SWEEPS, 2, cy, LANES), F32),
                pltpu.VMEM((SWEEPS, 2, nv, cx, cz), F32),
                pltpu.VMEM((SWEEPS, 2, nv, cx, cz), F32),
                pltpu.VMEM((SWEEPS, 2, nv, cy, cz), F32),
                pltpu.VMEM((2, nv, cx, cz), F32),
                pltpu.VMEM((2 * nv - 1, 1, LANES), F32),
                pltpu.VMEM((SWEEPS, n_span, slots, LANES), F32),
                pltpu.VMEM((SWEEPS, n_span, slots, LANES), F32),
                pltpu.VMEM((n_span, slots, LANES), F32),
                pltpu.VMEM((n_span, slots, LANES), F32),
                pltpu.VMEM((total, 2 * LANES), BF16),
                pltpu.VMEM((total, LANES), F32),
                pltpu.VMEM((nv, total, LANES), F32),
                pltpu.VMEM((LANES, 2 * total), BF16),
                pltpu.VMEM((total, LANES), F32),
                pltpu.VMEM((pairs, 2 * total, 2 * LANES), BF16),
                pltpu.VMEM((pairs, LANES, 2 * LANES), F32),
                dma((4,)),
                dma((SWEEPS, 6)),
                dma((SWEEPS, 6)),
                dma((SWEEPS, n_span)),
                dma((SWEEPS, n_span)),
                dma((n_span,)),
                dma((n_span,)),
            ],
            compiler_params=pltpu.CompilerParams(
                collective_id=0, has_side_effects=True, vmem_limit_bytes=48 * 1024 * 1024
            ),
            cost_estimate=pl.CostEstimate(
                flops=2 * SWEEPS * 6 * nv * nv * cx * cy * cz,
                bytes_accessed=4 * (3 * nv + 5) * cx * cy * cz,
                transcendentals=0,
            ),
        )(
            sensitivity, diagonal, face_coef, upper_blocks, lower_blocks, iface_blocks, production,
            send_cell, target_cell, orient, iface_weight,
        )

    grid = P(None, "chord", "span", "wall")
    rows = P("chord", "span", "wall", None, None)
    return jax.shard_map(
        local,
        mesh=mesh,
        in_specs=(grid, grid, grid, P(), P(), P(), P("chord", "span", "wall"), rows, rows, rows, rows),
        out_specs=(grid, P("chord", "span", "wall")),
        check_vma=False,
    )
```

```python
import functools

import jax
import jax.numpy as jnp
from jax import lax
from jax.experimental import pallas as pl
from jax.experimental.pallas import tpu as pltpu
from jax.sharding import PartitionSpec as P

SWEEPS = 3
LANES = 128
STEP = 2
MESH = pl.DeviceIdType.MESH
F32 = jnp.float32
BF16 = jnp.bfloat16


def iota(shape, dim):
    return lax.broadcasted_iota(jnp.int32, shape, dim)


def fiota(shape, dim):
    return iota(shape, dim).astype(F32)


def column(row, n):
    wide = jnp.broadcast_to(row.astype(F32), (n, n))
    return jnp.sum(jnp.where(iota((n, n), 0) == iota((n, n), 1), wide, 0.0), axis=1, keepdims=True)


def one_hots(cell):
    row = jnp.floor(cell * (1.0 / LANES))
    lane = fiota(cell.shape, 1)
    return jnp.where(row == lane, 1.0, 0.0), jnp.where(cell - row * LANES == lane, 1.0, 0.0)


def kernel(
    n_chord, n_span, n_wall, nv, cx, cy, slots,
    sens_hbm, diag_hbm, face_hbm, up_hbm, low_hbm, couple_hbm,
    send_hbm, target_hbm, orient_hbm, weight_hbm,
    out_hbm,
    up_ref, low_ref, couple_ref, send_ref, target_ref, orient_ref, weight_ref,
    sens, rdiag, face, adj, acc, halves,
    wall_out, wall_in, span_out, span_in, chord_in, span_term, wall_coef,
    iface_out, iface_in, cell_out, cell_in,
    pick_rows, pick_lanes, weights, put_rows, put_lanes, put_vals, put,
    load_sem, store_sem, halo_send, halo_recv, iface_send, iface_recv, cell_send, cell_recv,
):
    total = n_span * slots
    chunks = cx // STEP
    ci, si, wi = lax.axis_index("chord"), lax.axis_index("span"), lax.axis_index("wall")
    places = (("chord", ci, n_chord), ("span", si, n_span), ("wall", wi, n_wall))

    def exists(axis, side):
        _, place, count = places[axis]
        return place > 0 if side == 0 else place < count - 1

    def neighbour(axis, side):
        name, place, _ = places[axis]
        return {name: place - 1 if side == 0 else place + 1}

    loads = [
        pltpu.make_async_copy(src, dst, load_sem.at[k])
        for k, (src, dst) in enumerate(
            (
                (sens_hbm, sens), (diag_hbm, rdiag), (face_hbm, face),
                (up_hbm, up_ref), (low_hbm, low_ref), (couple_hbm, couple_ref),
                (send_hbm, send_ref), (target_hbm, target_ref),
                (orient_hbm, orient_ref), (weight_hbm, weight_ref),
            )
        )
    ]
    for load in loads:
        load.start()

    barrier = pltpu.get_barrier_semaphore()
    for axis in (0, 2):
        for side in (0, 1):
            @pl.when(exists(axis, side))
            def _():
                pl.semaphore_signal(
                    barrier, inc=1, device_id=neighbour(axis, side), device_id_type=MESH
                )
    peers = [lax.rem(si + d, n_span) for d in range(1, n_span)]
    for peer in peers:
        pl.semaphore_signal(barrier, inc=1, device_id={"span": peer}, device_id_type=MESH)

    for buf in range(SWEEPS):
        for j in range(nv):
            adj[buf, j, 0] = jnp.zeros((cy, LANES), F32)
            adj[buf, j, cx + 1] = jnp.zeros((cy, LANES), F32)
    for sweep in range(SWEEPS):
        for side in (0, 1):
            @pl.when(jnp.logical_not(exists(0, side)))
            def _():
                chord_in[sweep, side] = jnp.zeros(chord_in.shape[2:], F32)

            @pl.when(jnp.logical_not(exists(1, side)))
            def _():
                span_in[sweep, side] = jnp.zeros(span_in.shape[2:], F32)

            @pl.when(jnp.logical_not(exists(2, side)))
            def _():
                wall_in[sweep, side] = jnp.zeros(wall_in.shape[2:], F32)

    def cell_copy(peer, slot):
        return pltpu.make_async_remote_copy(
            src_ref=cell_out.at[peer], dst_ref=cell_in.at[slot],
            send_sem=cell_send.at[peer], recv_sem=cell_recv.at[slot],
            device_id={"span": peer}, device_id_type=MESH,
        )

    def halo_copy(sweep, axis, side):
        if axis == 0:
            src = adj.at[sweep, :, 1 if side == 0 else cx]
            dst = chord_in.at[sweep, 1 - side]
        elif axis == 1:
            src, dst = span_out.at[sweep, side], span_in.at[sweep, 1 - side]
        else:
            src, dst = wall_out.at[sweep], wall_in.at[sweep, 1 - side]
        return pltpu.make_async_remote_copy(
            src_ref=src, dst_ref=dst,
            send_sem=halo_send.at[sweep, 2 * axis + side],
            recv_sem=halo_recv.at[sweep, 2 * axis + 1 - side],
            device_id=neighbour(axis, side), device_id_type=MESH,
        )

    def each_halo(sweep, act):
        for axis in range(3):
            for side in (0, 1):
                @pl.when(exists(axis, side))
                def _():
                    act(axis, side)

    def start_halos(sweep):
        each_halo(sweep, lambda axis, side: halo_copy(sweep, axis, side).start())

    def wait_halos(sweep):
        each_halo(sweep, lambda axis, side: halo_copy(sweep, axis, 1 - side).wait_recv())

    def iface_copy(sweep, peer, slot):
        return pltpu.make_async_remote_copy(
            src_ref=iface_out.at[sweep, peer], dst_ref=iface_in.at[sweep, slot],
            send_sem=iface_send.at[sweep, peer], recv_sem=iface_recv.at[sweep, slot],
            device_id={"span": peer}, device_id_type=MESH,
        )

    lanes2d = iota((cy, LANES), 1)
    rows2d = iota((cy, LANES), 0)

    def keep(sweep, i, q, plane, value, packed):
        adj[sweep, i, plane + 1] = value
        high = value.astype(BF16)
        at = pl.multiple_of(plane * cy, cy)
        wide = pl.ds((i % 2) * LANES, LANES)
        halves[i // 2, pl.ds(at, cy), wide] = high
        halves[i // 2, pl.ds(cx * cy + at, cy), wide] = (value - high.astype(F32)).astype(BF16)
        span_out[sweep, 0, i, pl.ds(plane, 1)] = value[0:1]
        span_out[sweep, 1, i, pl.ds(plane, 1)] = value[cy - 1 : cy]
        pair = i * cx + plane
        turned = pltpu.roll(value, 2 * pair + 1, 1)
        return jnp.where(lanes2d // 2 == pair, turned, packed)

    def store(chunk):
        planes = pl.ds(chunk * STEP, STEP)
        return pltpu.make_async_copy(
            acc.at[:, planes], out_hbm.at[:, planes], store_sem.at[chunk]
        )

    loads[0].wait()
    loads[1].wait()

    def first(chunk, packed):
        for i in range(nv):
            for q in range(STEP):
                plane = chunk * STEP + q
                inverse = 1.0 / rdiag[i, plane]
                rdiag[i, plane] = inverse
                packed = keep(0, i, q, plane, sens[i, plane] * inverse, packed)
        return packed

    wall_out[0] = lax.fori_loop(0, chunks, first, jnp.zeros((cy, LANES), F32))
    greeted = n_span - 1
    for axis in (0, 2):
        for side in (0, 1):
            greeted = greeted + jnp.where(exists(axis, side), 1, 0)
    pl.semaphore_wait(barrier, greeted)
    start_halos(0)
    for k in range(3, 10):
        loads[k].wait()
    lane_id = iota((1, LANES), 1)
    for shift in range(-(nv - 1), nv):
        coef = jnp.zeros((1, LANES), F32)
        for i in range(nv):
            j = i + shift
            if 0 <= j < nv:
                mine = lane_id // (2 * cx) == i
                coef = jnp.where(mine & (lane_id % 2 == 0), up_ref[2, j, i], coef)
                coef = jnp.where(mine & (lane_id % 2 == 1), low_ref[2, j, i], coef)
        wall_coef[shift + nv - 1] = coef
    table = []
    for o in range(2):
        rows = []
        for j in range(nv):
            row = jnp.zeros((1, LANES), F32)
            for i in range(nv):
                row = jnp.where(lane_id == i, couple_ref[j, o, i], row)
            rows.append(row)
        table.append(rows)
    send_all = send_ref[0, 0, 0]
    target_all = target_ref[0, 0, 0]
    orient_all = orient_ref[0, 0, 0]
    weight_all = weight_ref[0, 0, 0]
    for t in range(n_span):
        part = pl.ds(t * slots, slots)
        cell_out[t] = jnp.broadcast_to(column(target_all[t : t + 1], slots), (slots, LANES))
        cell = jnp.broadcast_to(column(send_all[t : t + 1], slots), (slots, LANES))
        rows, lanes = one_hots(cell)
        pick_rows[part, 0:LANES] = rows.astype(BF16)
        pick_rows[part, LANES : 2 * LANES] = rows.astype(BF16)
        pick_lanes[part] = lanes
        facing = column(orient_all[t : t + 1], slots)
        weight = column(weight_all[t : t + 1], slots)
        for j in range(nv):
            weights[j, part] = weight * jnp.where(facing == 1.0, table[1][j], table[0][j])

    for peer in peers:
        cell_copy(peer, si).start()
    cell_in[si] = cell_out[si]
    loads[2].wait()

    for sweep in range(SWEEPS):
        values = jnp.zeros((total, LANES), F32)
        for pair in range(nv // 2):
            picked = jnp.dot(pick_rows[...], halves[pair], preferred_element_type=F32)
            for h in range(2):
                own = picked[:, h * LANES : (h + 1) * LANES] * pick_lanes[...]
                values = values + jnp.sum(own, axis=1, keepdims=True) * weights[2 * pair + h]
        for t in range(n_span):
            iface_out[sweep, t] = values[t * slots : (t + 1) * slots]
        for peer in peers:
            iface_copy(sweep, peer, si).start()
        iface_in[sweep, si] = iface_out[sweep, si]

        def own_part(chunk, carry):
            at = chunk * STEP
            for axis in range(3):
                sums = [None] * nv
                for j in range(nv):
                    if axis == 0:
                        low = adj[sweep, j, pl.ds(at, STEP)].reshape(STEP * cy, LANES)
                        up = adj[sweep, j, pl.ds(at + 2, STEP)].reshape(STEP * cy, LANES)
                    else:
                        here = adj[sweep, j, pl.ds(at + 1, STEP)]
                        if axis == 1:
                            low = jnp.concatenate([pltpu.roll(here[q], 1, 0) for q in range(STEP)])
                            up = jnp.concatenate(
                                [pltpu.roll(here[q], cy - 1, 0) for q in range(STEP)]
                            )
                        else:
                            here = here.reshape(STEP * cy, LANES)
                            low = pltpu.roll(here, 1, 1)
                            up = pltpu.roll(here, LANES - 1, 1)
                    for i in range(nv):
                        term = up_ref[axis, j, i] * up + low_ref[axis, j, i] * low
                        sums[i] = term if j == 0 else sums[i] + term
                scale = face[axis, pl.ds(at, STEP)].reshape(STEP * cy, LANES)
                for i in range(nv):
                    base = sens if axis == 0 else acc
                    rest = base[i, pl.ds(at, STEP)].reshape(STEP * cy, LANES) - scale * sums[i]
                    acc[i, pl.ds(at, STEP)] = rest.reshape(STEP, cy, LANES)
            return carry

        lax.fori_loop(0, chunks, own_part, 0)

        wait_halos(sweep)

        for side in (0, 1):
            blocks = low_ref if side == 0 else up_ref
            edge = 0 if side == 0 else cx - 1
            for i in range(nv):
                chord_sum = None
                span_sum = None
                for j in range(nv):
                    chord_new = blocks[0, j, i] * chord_in[sweep, side, j]
                    span_new = blocks[1, j, i] * (span_in[sweep, side, j] - span_out[sweep, 1 - side, j])
                    chord_sum = chord_new if j == 0 else chord_sum + chord_new
                    span_sum = span_new if j == 0 else span_sum + span_new
                acc[i, edge] = acc[i, edge] - face[0, edge] * chord_sum
                span_term[side, i] = span_sum
        from_low = pltpu.roll(wall_in[sweep, 0] - wall_out[sweep], 1, 1)
        from_high = pltpu.roll(wall_in[sweep, 1] - wall_out[sweep], LANES - 1, 1)
        edges = jnp.where(lanes2d % 2 == 0, from_high, from_low)
        wall_term = jnp.zeros((cy, LANES), F32)
        for shift in range(-(nv - 1), nv):
            moved = edges if shift == 0 else pltpu.roll(edges, (-2 * cx * shift) % LANES, 1)
            wall_term = wall_term + wall_coef[shift + nv - 1] * moved

        if sweep == 0:
            for peer in peers:
                cell_copy(peer, peer).wait_recv()
            rows, lanes = one_hots(cell_in[...].reshape(total, LANES))
            put_lanes[...] = lanes
            turned = jnp.transpose(rows).astype(BF16)
            put_rows[:, 0:total] = turned
            put_rows[:, total : 2 * total] = turned
        for peer in peers:
            iface_copy(sweep, peer, peer).wait_recv()
        arrived = iface_in[sweep].reshape(total, LANES)
        for i in range(nv):
            spread = arrived[:, i : i + 1] * put_lanes[...]
            high = spread.astype(BF16)
            wide = slice((i % 2) * LANES, (i % 2 + 1) * LANES)
            put_vals[i // 2, 0:total, wide] = high
            put_vals[i // 2, total : 2 * total, wide] = (spread - high.astype(F32)).astype(BF16)
        for pair in range(nv // 2):
            put[pair] = jnp.dot(put_rows[...], put_vals[pair], preferred_element_type=F32)

        def finish(chunk, packed):
            for q in range(STEP):
                plane = chunk * STEP + q
                at = pl.multiple_of(plane * cy, cy)
                for i in range(nv):
                    turn = lax.rem(2 * LANES - 1 - 2 * (i * cx + plane), LANES)
                    wall = pltpu.roll(wall_term, turn, 1)
                    wall = jnp.where((lanes2d == 0) | (lanes2d == LANES - 1), wall, 0.0)
                    span = jnp.where(rows2d == 0, span_term[0, i, pl.ds(plane, 1)], 0.0)
                    span = jnp.where(rows2d == cy - 1, span_term[1, i, pl.ds(plane, 1)], span)
                    rest = acc[i, plane] - face[1, plane] * span - face[2, plane] * wall
                    rest = rest - put[i // 2, pl.ds(at, cy), pl.ds((i % 2) * LANES, LANES)]
                    value = rest * rdiag[i, plane]
                    if sweep < SWEEPS - 1:
                        packed = keep(sweep + 1, i, q, plane, value, packed)
                    else:
                        acc[i, plane] = value
            if sweep == SWEEPS - 1:
                store(chunk).start()
            return packed

        packed = lax.fori_loop(0, chunks, finish, jnp.zeros((cy, LANES), F32))
        if sweep < SWEEPS - 1:
            wall_out[sweep + 1] = packed
            start_halos(sweep + 1)

    for chunk in range(chunks):
        store(chunk).wait()
    for peer in peers:
        cell_copy(peer, si).wait_send()
    for sweep in range(SWEEPS):
        each_halo(sweep, lambda axis, side: halo_copy(sweep, axis, side).wait_send())
        for peer in peers:
            iface_copy(sweep, peer, si).wait_send()


def solution(mesh):
    n_chord, n_span, n_wall = mesh.shape["chord"], mesh.shape["span"], mesh.shape["wall"]

    def local(
        sensitivity, diagonal, face_coef, upper_blocks, lower_blocks, iface_blocks, production,
        send_cell, target_cell, orient, iface_weight,
    ):
        nv, cx, cy, cz = sensitivity.shape
        slots = send_cell.shape[-1]
        total = n_span * slots
        pairs = nv // 2
        hbm = pl.BlockSpec(memory_space=pltpu.HBM)
        dma = pltpu.SemaphoreType.DMA
        field = (nv, cx, cy, cz)
        adjoint = pl.pallas_call(
            functools.partial(kernel, n_chord, n_span, n_wall, nv, cx, cy, slots),
            out_shape=jax.ShapeDtypeStruct(field, F32),
            in_specs=[hbm] * 10,
            out_specs=hbm,
            scratch_shapes=[
                pltpu.SMEM(upper_blocks.shape, F32),
                pltpu.SMEM(lower_blocks.shape, F32),
                pltpu.SMEM((nv, 2, nv), F32),
                pltpu.VMEM(send_cell.shape, jnp.int32),
                pltpu.VMEM(target_cell.shape, jnp.int32),
                pltpu.VMEM(orient.shape, jnp.int32),
                pltpu.VMEM(iface_weight.shape, F32),
                pltpu.VMEM(field, F32),
                pltpu.VMEM(field, F32),
                pltpu.VMEM((3, cx, cy, cz), F32),
                pltpu.VMEM((SWEEPS, nv, cx + 2, cy, cz), F32),
                pltpu.VMEM(field, F32),
                pltpu.VMEM((pairs, 2 * cx * cy, 2 * cz), BF16),
                pltpu.VMEM((SWEEPS, cy, LANES), F32),
                pltpu.VMEM((SWEEPS, 2, cy, LANES), F32),
                pltpu.VMEM((SWEEPS, 2, nv, cx, cz), F32),
                pltpu.VMEM((SWEEPS, 2, nv, cx, cz), F32),
                pltpu.VMEM((SWEEPS, 2, nv, cy, cz), F32),
                pltpu.VMEM((2, nv, cx, cz), F32),
                pltpu.VMEM((2 * nv - 1, 1, LANES), F32),
                pltpu.VMEM((SWEEPS, n_span, slots, LANES), F32),
                pltpu.VMEM((SWEEPS, n_span, slots, LANES), F32),
                pltpu.VMEM((n_span, slots, LANES), F32),
                pltpu.VMEM((n_span, slots, LANES), F32),
                pltpu.VMEM((total, 2 * LANES), BF16),
                pltpu.VMEM((total, LANES), F32),
                pltpu.VMEM((nv, total, LANES), F32),
                pltpu.VMEM((LANES, 2 * total), BF16),
                pltpu.VMEM((total, LANES), F32),
                pltpu.VMEM((pairs, 2 * total, 2 * LANES), BF16),
                pltpu.VMEM((pairs, LANES, 2 * LANES), F32),
                dma((10,)),
                dma((cx // STEP,)),
                dma((SWEEPS, 6)),
                dma((SWEEPS, 6)),
                dma((SWEEPS, n_span)),
                dma((SWEEPS, n_span)),
                dma((n_span,)),
                dma((n_span,)),
            ],
            compiler_params=pltpu.CompilerParams(
                collective_id=0, has_side_effects=True, vmem_limit_bytes=125 * 512 * 1024
            ),
            cost_estimate=pl.CostEstimate(
                flops=2 * SWEEPS * 6 * nv * nv * cx * cy * cz,
                bytes_accessed=4 * (3 * nv + 5) * cx * cy * cz,
                transcendentals=0,
            ),
        )(
            sensitivity, diagonal, face_coef, upper_blocks, lower_blocks,
            iface_blocks.transpose(1, 0, 2), send_cell, target_cell, orient, iface_weight,
        )
        return adjoint, production * adjoint[nv - 1]

    grid = P(None, "chord", "span", "wall")
    rows = P("chord", "span", "wall", None, None)
    return jax.shard_map(
        local,
        mesh=mesh,
        in_specs=(grid, grid, grid, P(), P(), P(), P("chord", "span", "wall"), rows, rows, rows, rows),
        out_specs=(grid, P("chord", "span", "wall")),
        check_vma=False,
    )
```

```python
import functools

import jax
import jax.numpy as jnp
from jax import lax
from jax.experimental import pallas as pl
from jax.experimental.pallas import tpu as pltpu
from jax.sharding import PartitionSpec as P

SWEEPS = 3
LANES = 128
STEP = 2
MESH = pl.DeviceIdType.MESH
F32 = jnp.float32
BF16 = jnp.bfloat16


def iota(shape, dim):
    return lax.broadcasted_iota(jnp.int32, shape, dim)


def fiota(shape, dim):
    return iota(shape, dim).astype(F32)


def column(row, n):
    wide = jnp.broadcast_to(row.astype(F32), (n, n))
    return jnp.sum(jnp.where(iota((n, n), 0) == iota((n, n), 1), wide, 0.0), axis=1, keepdims=True)


def one_hots(cell):
    row = jnp.floor(cell * (1.0 / LANES))
    lane = fiota(cell.shape, 1)
    return jnp.where(row == lane, 1.0, 0.0), jnp.where(cell - row * LANES == lane, 1.0, 0.0)


def kernel(
    n_chord, n_span, n_wall, nv, cx, cy, slots,
    sens_hbm, diag_hbm, face_hbm, up_hbm, low_hbm, couple_hbm, prod_hbm,
    send_hbm, target_hbm, orient_hbm, weight_hbm,
    out_hbm, grad_hbm,
    up_ref, low_ref, couple_ref, send_ref, target_ref, orient_ref, weight_ref,
    sens, rdiag, face, prod, adj, acc, halves,
    wall_out, wall_in, span_out, span_in, chord_in, span_term, wall_coef,
    iface_out, iface_in, cell_out, cell_in,
    pick_rows, pick_lanes, weights, put_rows, put_lanes, put_vals, put,
    load_sem, store_sem, grad_sem, halo_send, halo_recv, iface_send, iface_recv, cell_send, cell_recv,
):
    total = n_span * slots
    chunks = cx // STEP
    ci, si, wi = lax.axis_index("chord"), lax.axis_index("span"), lax.axis_index("wall")
    places = (("chord", ci, n_chord), ("span", si, n_span), ("wall", wi, n_wall))

    def exists(axis, side):
        _, place, count = places[axis]
        return place > 0 if side == 0 else place < count - 1

    def neighbour(axis, side):
        name, place, _ = places[axis]
        return {name: place - 1 if side == 0 else place + 1}

    loads = [
        pltpu.make_async_copy(src, dst, load_sem.at[k])
        for k, (src, dst) in enumerate(
            (
                (sens_hbm, sens), (diag_hbm, rdiag), (face_hbm, face),
                (up_hbm, up_ref), (low_hbm, low_ref), (couple_hbm, couple_ref),
                (send_hbm, send_ref), (target_hbm, target_ref),
                (orient_hbm, orient_ref), (weight_hbm, weight_ref),
                (prod_hbm, prod),
            )
        )
    ]
    for load in loads:
        load.start()

    barrier = pltpu.get_barrier_semaphore()
    for axis in (0, 2):
        for side in (0, 1):
            @pl.when(exists(axis, side))
            def _():
                pl.semaphore_signal(
                    barrier, inc=1, device_id=neighbour(axis, side), device_id_type=MESH
                )
    peers = [lax.rem(si + d, n_span) for d in range(1, n_span)]
    for peer in peers:
        pl.semaphore_signal(barrier, inc=1, device_id={"span": peer}, device_id_type=MESH)

    for buf in range(SWEEPS):
        for j in range(nv):
            adj[buf, j, 0] = jnp.zeros((cy, LANES), F32)
            adj[buf, j, cx + 1] = jnp.zeros((cy, LANES), F32)
    for sweep in range(SWEEPS):
        for side in (0, 1):
            @pl.when(jnp.logical_not(exists(0, side)))
            def _():
                chord_in[sweep, side] = jnp.zeros(chord_in.shape[2:], F32)

            @pl.when(jnp.logical_not(exists(1, side)))
            def _():
                span_in[sweep, side] = jnp.zeros(span_in.shape[2:], F32)

            @pl.when(jnp.logical_not(exists(2, side)))
            def _():
                wall_in[sweep, side] = jnp.zeros(wall_in.shape[2:], F32)

    def cell_copy(peer, slot):
        return pltpu.make_async_remote_copy(
            src_ref=cell_out.at[peer], dst_ref=cell_in.at[slot],
            send_sem=cell_send.at[peer], recv_sem=cell_recv.at[slot],
            device_id={"span": peer}, device_id_type=MESH,
        )

    def halo_copy(sweep, axis, side):
        if axis == 0:
            src = adj.at[sweep, :, 1 if side == 0 else cx]
            dst = chord_in.at[sweep, 1 - side]
        elif axis == 1:
            src, dst = span_out.at[sweep, side], span_in.at[sweep, 1 - side]
        else:
            src, dst = wall_out.at[sweep], wall_in.at[sweep, 1 - side]
        return pltpu.make_async_remote_copy(
            src_ref=src, dst_ref=dst,
            send_sem=halo_send.at[sweep, 2 * axis + side],
            recv_sem=halo_recv.at[sweep, 2 * axis + 1 - side],
            device_id=neighbour(axis, side), device_id_type=MESH,
        )

    def each_halo(sweep, act):
        for axis in range(3):
            for side in (0, 1):
                @pl.when(exists(axis, side))
                def _():
                    act(axis, side)

    def start_halos(sweep):
        each_halo(sweep, lambda axis, side: halo_copy(sweep, axis, side).start())

    def wait_halos(sweep):
        each_halo(sweep, lambda axis, side: halo_copy(sweep, axis, 1 - side).wait_recv())

    def iface_copy(sweep, peer, slot):
        return pltpu.make_async_remote_copy(
            src_ref=iface_out.at[sweep, peer], dst_ref=iface_in.at[sweep, slot],
            send_sem=iface_send.at[sweep, peer], recv_sem=iface_recv.at[sweep, slot],
            device_id={"span": peer}, device_id_type=MESH,
        )

    lanes2d = iota((cy, LANES), 1)
    rows2d = iota((cy, LANES), 0)

    def keep(sweep, i, q, plane, value, packed):
        adj[sweep, i, plane + 1] = value
        high = value.astype(BF16)
        at = pl.multiple_of(plane * cy, cy)
        wide = pl.ds((i % 2) * LANES, LANES)
        halves[i // 2, pl.ds(at, cy), wide] = high
        halves[i // 2, pl.ds(cx * cy + at, cy), wide] = (value - high.astype(F32)).astype(BF16)
        span_out[sweep, 0, i, pl.ds(plane, 1)] = value[0:1]
        span_out[sweep, 1, i, pl.ds(plane, 1)] = value[cy - 1 : cy]
        pair = i * cx + plane
        turned = pltpu.roll(value, 2 * pair + 1, 1)
        return jnp.where(lanes2d // 2 == pair, turned, packed)

    def store(chunk):
        planes = pl.ds(chunk * STEP, STEP)
        return (
            pltpu.make_async_copy(prod.at[planes], grad_hbm.at[planes], grad_sem.at[chunk]),
            pltpu.make_async_copy(acc.at[:, planes], out_hbm.at[:, planes], store_sem.at[chunk]),
        )

    loads[0].wait()
    loads[1].wait()

    def first(chunk, packed):
        for i in range(nv):
            for q in range(STEP):
                plane = chunk * STEP + q
                inverse = 1.0 / rdiag[i, plane]
                rdiag[i, plane] = inverse
                packed = keep(0, i, q, plane, sens[i, plane] * inverse, packed)
        return packed

    wall_out[0] = lax.fori_loop(0, chunks, first, jnp.zeros((cy, LANES), F32))
    greeted = n_span - 1
    for axis in (0, 2):
        for side in (0, 1):
            greeted = greeted + jnp.where(exists(axis, side), 1, 0)
    pl.semaphore_wait(barrier, greeted)
    start_halos(0)
    for k in range(3, 10):
        loads[k].wait()
    lane_id = iota((1, LANES), 1)
    for shift in range(-(nv - 1), nv):
        coef = jnp.zeros((1, LANES), F32)
        for i in range(nv):
            j = i + shift
            if 0 <= j < nv:
                mine = lane_id // (2 * cx) == i
                coef = jnp.where(mine & (lane_id % 2 == 0), up_ref[2, j, i], coef)
                coef = jnp.where(mine & (lane_id % 2 == 1), low_ref[2, j, i], coef)
        wall_coef[shift + nv - 1] = coef
    table = []
    for o in range(2):
        rows = []
        for j in range(nv):
            row = jnp.zeros((1, LANES), F32)
            for i in range(nv):
                row = jnp.where(lane_id == i, couple_ref[j, o, i], row)
            rows.append(row)
        table.append(rows)
    send_all = send_ref[0, 0, 0]
    target_all = target_ref[0, 0, 0]
    orient_all = orient_ref[0, 0, 0]
    weight_all = weight_ref[0, 0, 0]
    for t in range(n_span):
        part = pl.ds(t * slots, slots)
        cell_out[t] = jnp.broadcast_to(column(target_all[t : t + 1], slots), (slots, LANES))
        cell = jnp.broadcast_to(column(send_all[t : t + 1], slots), (slots, LANES))
        rows, lanes = one_hots(cell)
        pick_rows[part, 0:LANES] = rows.astype(BF16)
        pick_rows[part, LANES : 2 * LANES] = rows.astype(BF16)
        pick_lanes[part] = lanes
        facing = column(orient_all[t : t + 1], slots)
        weight = column(weight_all[t : t + 1], slots)
        for j in range(nv):
            weights[j, part] = weight * jnp.where(facing == 1.0, table[1][j], table[0][j])

    for peer in peers:
        cell_copy(peer, si).start()
    cell_in[si] = cell_out[si]
    loads[2].wait()

    for sweep in range(SWEEPS):
        values = jnp.zeros((total, LANES), F32)
        for pair in range(nv // 2):
            picked = jnp.dot(pick_rows[...], halves[pair], preferred_element_type=F32)
            for h in range(2):
                own = picked[:, h * LANES : (h + 1) * LANES] * pick_lanes[...]
                values = values + jnp.sum(own, axis=1, keepdims=True) * weights[2 * pair + h]
        for t in range(n_span):
            iface_out[sweep, t] = values[t * slots : (t + 1) * slots]
        for peer in peers:
            iface_copy(sweep, peer, si).start()
        iface_in[sweep, si] = iface_out[sweep, si]

        def own_part(chunk, carry):
            at = chunk * STEP
            for axis in range(3):
                sums = [None] * nv
                for j in range(nv):
                    if axis == 0:
                        low = adj[sweep, j, pl.ds(at, STEP)].reshape(STEP * cy, LANES)
                        up = adj[sweep, j, pl.ds(at + 2, STEP)].reshape(STEP * cy, LANES)
                    else:
                        here = adj[sweep, j, pl.ds(at + 1, STEP)]
                        if axis == 1:
                            low = jnp.concatenate([pltpu.roll(here[q], 1, 0) for q in range(STEP)])
                            up = jnp.concatenate(
                                [pltpu.roll(here[q], cy - 1, 0) for q in range(STEP)]
                            )
                        else:
                            here = here.reshape(STEP * cy, LANES)
                            low = pltpu.roll(here, 1, 1)
                            up = pltpu.roll(here, LANES - 1, 1)
                    for i in range(nv):
                        term = up_ref[axis, j, i] * up + low_ref[axis, j, i] * low
                        sums[i] = term if j == 0 else sums[i] + term
                scale = face[axis, pl.ds(at, STEP)].reshape(STEP * cy, LANES)
                for i in range(nv):
                    base = sens if axis == 0 else acc
                    rest = base[i, pl.ds(at, STEP)].reshape(STEP * cy, LANES) - scale * sums[i]
                    acc[i, pl.ds(at, STEP)] = rest.reshape(STEP, cy, LANES)
            return carry

        lax.fori_loop(0, chunks, own_part, 0)

        wait_halos(sweep)

        for side in (0, 1):
            blocks = low_ref if side == 0 else up_ref
            edge = 0 if side == 0 else cx - 1
            for i in range(nv):
                chord_sum = None
                span_sum = None
                for j in range(nv):
                    chord_new = blocks[0, j, i] * chord_in[sweep, side, j]
                    span_new = blocks[1, j, i] * (span_in[sweep, side, j] - span_out[sweep, 1 - side, j])
                    chord_sum = chord_new if j == 0 else chord_sum + chord_new
                    span_sum = span_new if j == 0 else span_sum + span_new
                acc[i, edge] = acc[i, edge] - face[0, edge] * chord_sum
                span_term[side, i] = span_sum
        from_low = pltpu.roll(wall_in[sweep, 0] - wall_out[sweep], 1, 1)
        from_high = pltpu.roll(wall_in[sweep, 1] - wall_out[sweep], LANES - 1, 1)
        edges = jnp.where(lanes2d % 2 == 0, from_high, from_low)
        wall_term = jnp.zeros((cy, LANES), F32)
        for shift in range(-(nv - 1), nv):
            moved = edges if shift == 0 else pltpu.roll(edges, (-2 * cx * shift) % LANES, 1)
            wall_term = wall_term + wall_coef[shift + nv - 1] * moved

        if sweep == 0:
            for peer in peers:
                cell_copy(peer, peer).wait_recv()
            rows, lanes = one_hots(cell_in[...].reshape(total, LANES))
            put_lanes[...] = lanes
            turned = jnp.transpose(rows).astype(BF16)
            put_rows[:, 0:total] = turned
            put_rows[:, total : 2 * total] = turned
        for peer in peers:
            iface_copy(sweep, peer, peer).wait_recv()
        arrived = iface_in[sweep].reshape(total, LANES)
        for i in range(nv):
            spread = arrived[:, i : i + 1] * put_lanes[...]
            high = spread.astype(BF16)
            wide = slice((i % 2) * LANES, (i % 2 + 1) * LANES)
            put_vals[i // 2, 0:total, wide] = high
            put_vals[i // 2, total : 2 * total, wide] = (spread - high.astype(F32)).astype(BF16)
        for pair in range(nv // 2):
            put[pair] = jnp.dot(put_rows[...], put_vals[pair], preferred_element_type=F32)

        def finish(chunk, packed):
            for q in range(STEP):
                plane = chunk * STEP + q
                at = pl.multiple_of(plane * cy, cy)
                for i in range(nv):
                    turn = lax.rem(2 * LANES - 1 - 2 * (i * cx + plane), LANES)
                    wall = pltpu.roll(wall_term, turn, 1)
                    wall = jnp.where((lanes2d == 0) | (lanes2d == LANES - 1), wall, 0.0)
                    span = jnp.where(rows2d == 0, span_term[0, i, pl.ds(plane, 1)], 0.0)
                    span = jnp.where(rows2d == cy - 1, span_term[1, i, pl.ds(plane, 1)], span)
                    rest = acc[i, plane] - face[1, plane] * span - face[2, plane] * wall
                    rest = rest - put[i // 2, pl.ds(at, cy), pl.ds((i % 2) * LANES, LANES)]
                    value = rest * rdiag[i, plane]
                    if sweep < SWEEPS - 1:
                        packed = keep(sweep + 1, i, q, plane, value, packed)
                    else:
                        acc[i, plane] = value
                        if i == nv - 1:
                            prod[plane] = prod[plane] * value
            if sweep == SWEEPS - 1:
                for copy in store(chunk):
                    copy.start()
            return packed

        if sweep == SWEEPS - 1:
            loads[10].wait()
        packed = lax.fori_loop(0, chunks, finish, jnp.zeros((cy, LANES), F32))
        if sweep < SWEEPS - 1:
            wall_out[sweep + 1] = packed
            start_halos(sweep + 1)

    for chunk in range(chunks):
        for copy in store(chunk):
            copy.wait()
    for peer in peers:
        cell_copy(peer, si).wait_send()
    for sweep in range(SWEEPS):
        each_halo(sweep, lambda axis, side: halo_copy(sweep, axis, side).wait_send())
        for peer in peers:
            iface_copy(sweep, peer, si).wait_send()


def solution(mesh):
    n_chord, n_span, n_wall = mesh.shape["chord"], mesh.shape["span"], mesh.shape["wall"]

    def local(
        sensitivity, diagonal, face_coef, upper_blocks, lower_blocks, iface_blocks, production,
        send_cell, target_cell, orient, iface_weight,
    ):
        nv, cx, cy, cz = sensitivity.shape
        slots = send_cell.shape[-1]
        total = n_span * slots
        pairs = nv // 2
        hbm = pl.BlockSpec(memory_space=pltpu.HBM)
        dma = pltpu.SemaphoreType.DMA
        field = (nv, cx, cy, cz)
        return pl.pallas_call(
            functools.partial(kernel, n_chord, n_span, n_wall, nv, cx, cy, slots),
            out_shape=(
                jax.ShapeDtypeStruct(field, F32),
                jax.ShapeDtypeStruct((cx, cy, cz), F32),
            ),
            in_specs=[hbm] * 11,
            out_specs=(hbm, hbm),
            scratch_shapes=[
                pltpu.SMEM(upper_blocks.shape, F32),
                pltpu.SMEM(lower_blocks.shape, F32),
                pltpu.SMEM((nv, 2, nv), F32),
                pltpu.VMEM(send_cell.shape, jnp.int32),
                pltpu.VMEM(target_cell.shape, jnp.int32),
                pltpu.VMEM(orient.shape, jnp.int32),
                pltpu.VMEM(iface_weight.shape, F32),
                pltpu.VMEM(field, F32),
                pltpu.VMEM(field, F32),
                pltpu.VMEM((3, cx, cy, cz), F32),
                pltpu.VMEM((cx, cy, cz), F32),
                pltpu.VMEM((SWEEPS, nv, cx + 2, cy, cz), F32),
                pltpu.VMEM(field, F32),
                pltpu.VMEM((pairs, 2 * cx * cy, 2 * cz), BF16),
                pltpu.VMEM((SWEEPS, cy, LANES), F32),
                pltpu.VMEM((SWEEPS, 2, cy, LANES), F32),
                pltpu.VMEM((SWEEPS, 2, nv, cx, cz), F32),
                pltpu.VMEM((SWEEPS, 2, nv, cx, cz), F32),
                pltpu.VMEM((SWEEPS, 2, nv, cy, cz), F32),
                pltpu.VMEM((2, nv, cx, cz), F32),
                pltpu.VMEM((2 * nv - 1, 1, LANES), F32),
                pltpu.VMEM((SWEEPS, n_span, slots, LANES), F32),
                pltpu.VMEM((SWEEPS, n_span, slots, LANES), F32),
                pltpu.VMEM((n_span, slots, LANES), F32),
                pltpu.VMEM((n_span, slots, LANES), F32),
                pltpu.VMEM((total, 2 * LANES), BF16),
                pltpu.VMEM((total, LANES), F32),
                pltpu.VMEM((nv, total, LANES), F32),
                pltpu.VMEM((LANES, 2 * total), BF16),
                pltpu.VMEM((total, LANES), F32),
                pltpu.VMEM((pairs, 2 * total, 2 * LANES), BF16),
                pltpu.VMEM((pairs, LANES, 2 * LANES), F32),
                dma((11,)),
                dma((cx // STEP,)),
                dma((cx // STEP,)),
                dma((SWEEPS, 6)),
                dma((SWEEPS, 6)),
                dma((SWEEPS, n_span)),
                dma((SWEEPS, n_span)),
                dma((n_span,)),
                dma((n_span,)),
            ],
            compiler_params=pltpu.CompilerParams(
                collective_id=0, has_side_effects=True, vmem_limit_bytes=125 * 512 * 1024
            ),
            cost_estimate=pl.CostEstimate(
                flops=2 * SWEEPS * 6 * nv * nv * cx * cy * cz,
                bytes_accessed=4 * (3 * nv + 5) * cx * cy * cz,
                transcendentals=0,
            ),
        )(
            sensitivity, diagonal, face_coef, upper_blocks, lower_blocks,
            iface_blocks.transpose(1, 0, 2), production,
            send_cell, target_cell, orient, iface_weight,
        )

    grid = P(None, "chord", "span", "wall")
    rows = P("chord", "span", "wall", None, None)
    return jax.shard_map(
        local,
        mesh=mesh,
        in_specs=(grid, grid, grid, P(), P(), P(), P("chord", "span", "wall"), rows, rows, rows, rows),
        out_specs=(grid, P("chord", "span", "wall")),
        check_vma=False,
    )
```
